128 devices in a mesh: circ: 16 (over z_hi, y, core), xsec: 8 (over z_lo, x).
Axes of the slice: x: 4, y: 4, z: 4 (z_hi: 2, z_lo: 2; z = z_hi * 2 + z_lo), core: 2. Of those that a mesh axis runs over, the one named last changes fastest.
Arguments:
- displacement: float32 [3, 6291456], P(None, ('circ', 'xsec')), may hold values from -2 to 2
- velocity: float32 [3, 6291456], P(None, ('circ', 'xsec')), may hold values from -2 to 2
- load: float32 [3, 6291456], P(None, ('circ', 'xsec')), may hold values from -3 to 3
- mass: float32 [6291456], P(('circ', 'xsec')), may hold values from 1 to 4
- stiffness: float32 [64, 64, 131072], P(None, None, ('circ', 'xsec')), may hold values from -0.4 to 4.5
- connectivity: int32 [64, 131072], P(None, ('circ', 'xsec')), may hold values from 0 to 51199, as said below
- clearance: float32 [16384, 128], P(('circ', 'xsec')), may hold values from -0.3 to 0.3
- match_device: int32 [4, 16384, 1], P(None, ('circ', 'xsec')), may hold values from 0 to 127; in each aligned block of 128 rows (0 to 127, 128 to 255, ..., all dimensions but the last counted through in order) at most 2 rows name the same one
- match_slot: int32 [4, 16384], P(None, ('circ', 'xsec')), may hold values from 0 to 127
Outputs:
- final_displacement: float32 [3, 6291456], P(None, ('circ', 'xsec'))
- final_velocity: float32 [3, 6291456], P(None, ('circ', 'xsec'))
The draws below stay inside these ranges and needn't reach their ends.
Inputs may be any that keep to these rules, and one draw needn't show every extreme that they name: `match_device`: in every step, at most 2 of one device's 128 cycle blocks name the same device, and some device's blocks name one device exactly 2 times. `connectivity`: all nodes of one element block lie in one aligned run of 64 extended nodes (indices t * 64 to t * 64 + 63 for some t).
All inputs are finite; a program needn't handle non-finite values.
Results may differ from the reference program's by a relative error of at most 0.0001.
Values sent between devices are 32-bit elements; how exact they have to be, the bound alone decides.
A program may use at most 192 MiB of HBM per device.

```python
import math
import jax
import jax.numpy as jnp
import numpy as np
from jax import lax

NODES_DEV = 49152
BLOCKS_DEV = 1024
FACE = 1024
SURF_DEV = 128
SURF_NODES = 128
BLOCK = 64
STEPS = 4
CAP = 2
NODES = 6291456
ELEMS = 131072
SURF_ALL = 16384
N_CIRC = 16
N_XSEC = 8
DEVICES = 128


def draw_stiffness(key, part):
    key = jax.random.fold_in(key, 11)
    first, second = jax.random.split(key)
    offdiag = jnp.clip(0.1 * jax.random.normal(first, (BLOCK, BLOCK, ELEMS), jnp.float32), -0.4, 0.4)
    diagonal = jax.random.uniform(second, (BLOCK, ELEMS), jnp.float32, 2.0, 4.0)
    rows = jnp.arange(BLOCK)
    on_diag = (rows[:, None] == rows[None, :])[:, :, None]
    return jnp.where(on_diag, diagonal[:, None, :] + 0.0 * offdiag, offdiag)


def draw_connectivity(key, part):
    key = jax.random.fold_in(key, 23)
    first, second = jax.random.split(key)
    tile_count = (NODES_DEV + 2 * FACE) // BLOCK
    tiles = jax.random.randint(first, (ELEMS,), 0, tile_count, jnp.int32)
    local = jax.random.randint(second, (BLOCK, ELEMS), 0, BLOCK, jnp.int32)
    return (tiles[None, :] * BLOCK + local).astype(jnp.int32)


def plant(drawn, rng, smallest, largest):
    dims = drawn.shape
    spot = [jax.random.randint(jax.random.fold_in(rng, axis), (), 0, dims[axis]) for axis in range(len(dims))]
    drawn = drawn.at[tuple(spot)].set(smallest)
    longest = dims.index(max(dims))
    spot[longest] = (spot[longest] + 1) % dims[longest]
    return drawn.at[tuple(spot)].set(largest)


def levels(rng, dims, cuts, smallest, top_value):
    level, own = 1.0, jax.random.fold_in(rng, 6)
    for axis_at, blocks in cuts:
        steps = jnp.exp(jax.random.uniform(jax.random.fold_in(own, axis_at), (blocks,), jnp.float32, smallest / len(cuts), top_value / len(cuts)))
        level = level * jnp.repeat(steps, dims[axis_at] // blocks).reshape([-1 if axis == axis_at else 1 for axis in range(len(dims))])
    return level


def assign_block(rng, own, number, rows, number_of, top, reach, slope):
    order = jax.random.permutation(rng, number_of)
    heavy_load, ordinary = load_shares(number_of, rows * top, reach, slope, True), load_shares(number_of, rows * top, reach, slope, False)
    places = jnp.arange(number_of)

    def named(tallies, turn):
        used = int((tallies > 0).sum())
        fixed = max(1, used // 4)
        shifted = fixed + (places - fixed + turn * (used - fixed)) % max(1, number_of - fixed)
        return jnp.zeros((number_of,), jnp.int32).at[order[jnp.where(places < fixed, places, shifted)]].set(jnp.asarray(tallies, jnp.int32))

    tallies = jnp.where(number % 4 == 0, named(heavy_load, number // 4), named(ordinary, number - number // 4 - 1))
    mixed = jax.random.permutation(jax.random.fold_in(own, 3), number_of)
    donor, taker = mixed[0:number_of // 2 * 2:2], mixed[1:number_of // 2 * 2:2]
    slack = jnp.minimum(tallies[donor] - 1, reach - tallies[taker]) // 2
    slack = jnp.where((donor == order[0]) | (taker == order[0]) | (tallies[taker] == 0), 0, jnp.maximum(slack, 0))
    shifted = jax.random.randint(jax.random.fold_in(own, 4), (number_of // 2,), 0, 1 << 20) % (slack + 1)
    tallies = tallies.at[donor].add(-shifted).at[taker].add(shifted)
    labels = jnp.searchsorted(jnp.cumsum(tallies), jnp.arange(rows * top), side="right").astype(jnp.int32)
    listing = labels.reshape(top, rows).T
    listing = listing[jax.random.permutation(jax.random.fold_in(own, 1), rows)]
    turn = jax.random.randint(jax.random.fold_in(own, 2), (rows, 1), 0, top)
    return jnp.take_along_axis(listing, (jnp.arange(top)[None, :] + turn) % top, axis=1)


def load_shares(count, total, reach, skew, full):
    portions = [(1 << 20) // math.isqrt(grade ** skew) + 1 for grade in range(1, count + 1)]
    largest = reach if full else min(reach, max(-(-total // count), total * portions[0] // sum(portions)))
    least = 1 if total - largest >= count - 1 else 0
    given, rest = [largest] + [least] * (count - 1), total - largest - least * (count - 1)
    while rest > 0:
        free = [i for i in range(1, count) if given[i] < largest] or [i for i in range(1, count) if given[i] < reach]
        whole, budget = sum([portions[i] for i in free]), rest
        for i in free:
            extra = min(reach - given[i], max(1, budget * portions[i] // whole), rest)
            given[i] = given[i] + extra
            rest = rest - extra
    return np.array(given)


def scatter_about(key, dims, scale, most, cuts=(), kind=jnp.bfloat16):
    drawn = scale * jax.random.normal(key, dims, jnp.float32)
    if cuts:
        drawn = drawn * levels(key, dims, cuts, -0.22, 0.18)
    return jnp.clip(drawn, -most, most).astype(kind)


def setup_inputs(seed: int = 0) -> dict:
    seeds = jax.random.split(jax.random.key(seed), 10)
    displacement = scatter_about(seeds[0], (3, NODES), 0.3, 2.0, ((1, 128),), jnp.float32)
    velocity = scatter_about(seeds[1], (3, NODES), 0.3, 2.0, ((1, 128),), jnp.float32)
    load = scatter_about(seeds[2], (3, NODES), 0.5, 3.0, ((1, 128),), jnp.float32)
    mass = jnp.clip(jnp.exp(math.log(4.0) - 1.3862944 * jax.random.uniform(seeds[3], (NODES,), jnp.float32) ** levels(seeds[3], (NODES,), ((0, 128),), -0.2, 0.2)), 1.0, 4.0)
    stiffness = draw_stiffness(jax.random.fold_in(seeds[9], 71), 0)
    connectivity = draw_connectivity(jax.random.fold_in(seeds[9], 71), 0)
    clearance = jnp.clip(jax.random.uniform(seeds[6], (SURF_ALL, SURF_NODES), jnp.float32, -0.3, 0.3) * levels(seeds[6], (SURF_ALL, SURF_NODES), ((0, 128),), -0.4, 0.0), -0.3, 0.3)
    match_device_keys = jax.random.split(jax.random.fold_in(seeds[7], 1), STEPS * SURF_ALL // SURF_DEV)
    match_device_turns = jax.random.permutation(jax.random.fold_in(seeds[7], 3), STEPS * SURF_ALL // SURF_DEV)
    match_device = jax.vmap(lambda own, number: assign_block(jax.random.fold_in(seeds[7], 2), own, number, SURF_DEV, DEVICES, 1, CAP, 2))(match_device_keys, match_device_turns).reshape((STEPS, SURF_ALL, 1))
    match_slot = plant(jax.random.randint(seeds[8], (STEPS, SURF_ALL), 0, SURF_DEV), jax.random.fold_in(seeds[8], 1), 0, SURF_DEV - 1).astype(jnp.int32)
    return dict(displacement=displacement, velocity=velocity, load=load, mass=mass, stiffness=stiffness, connectivity=connectivity, clearance=clearance, match_device=match_device, match_slot=match_slot)


PENALTY = 4.0
DASHPOT = 1.0
FRICTION = 2.0
TIMESTEP = 0.25


def contact_terms(cycle_disp, cycle_move, groove_disp, groove_move, clear):
    relative = [cycle_disp[k] - groove_disp[k] for k in range(3)]
    intersection = jnp.maximum(relative[0] - clear, 0.0)
    closing = cycle_move[0] - groove_move[0]
    return [intersection * (PENALTY + DASHPOT * closing), FRICTION * intersection * relative[1], FRICTION * intersection * relative[2]]


def block_forces(extended, stiff, links):
    gathered = extended[:, links]
    product = jnp.einsum('ije,cje->cie', stiff, gathered, precision=lax.Precision.HIGHEST)
    return jnp.zeros_like(extended).at[:, links].add(product)


def reference(displacement, velocity, load, mass, stiffness, connectivity, clearance, match_device, match_slot):
    devices = N_CIRC * N_XSEC
    own = NODES_DEV
    face = FACE
    surface = SURF_DEV * SURF_NODES
    groove_start = own - surface
    stiff_dev = stiffness.reshape(BLOCK, BLOCK, devices, BLOCKS_DEV)
    links_dev = connectivity.reshape(BLOCK, devices, BLOCKS_DEV)
    deform = displacement
    motion = velocity
    for step_index in range(STEPS):
        quad = deform.reshape(3, N_CIRC, N_XSEC, own)
        before = jnp.roll(quad[..., own - face:], 1, axis=1)
        after = jnp.roll(quad[..., :face], -1, axis=1)
        extended = jnp.concatenate([before, quad, after], axis=-1).reshape(3, devices, own + 2 * face)
        summed = jax.vmap(block_forces, in_axes=(1, 2, 1), out_axes=1)(extended, stiff_dev, links_dev)
        summed = summed.reshape(3, N_CIRC, N_XSEC, own + 2 * face)
        internal = summed[..., face:face + own]
        internal = internal.at[..., own - face:].add(jnp.roll(summed[..., :face], -1, axis=1))
        internal = internal.at[..., :face].add(jnp.roll(summed[..., face + own:], 1, axis=1))
        per_dev = deform.reshape(3, devices, own)
        move_dev = motion.reshape(3, devices, own)
        cycle_disp = per_dev[:, :, :surface].reshape(3, devices * SURF_DEV, SURF_NODES)
        cycle_move = move_dev[:, :, :surface].reshape(3, devices * SURF_DEV, SURF_NODES)
        groove_disp = per_dev[:, :, groove_start:].reshape(3, devices * SURF_DEV, SURF_NODES)
        groove_move = move_dev[:, :, groove_start:].reshape(3, devices * SURF_DEV, SURF_NODES)
        target = (match_device[step_index, :, 0] * SURF_DEV + match_slot[step_index]).astype(jnp.int32)
        terms = contact_terms(cycle_disp, cycle_move, groove_disp[:, target], groove_move[:, target], clearance[target])
        pair_force = jnp.stack(terms, axis=0)
        groove_force = jnp.zeros((3, devices * SURF_DEV, SURF_NODES), jnp.float32).at[:, target].add(pair_force)
        contact = jnp.zeros((3, devices, own), jnp.float32)
        contact = contact.at[:, :, :surface].add(-pair_force.reshape(3, devices, surface))
        contact = contact.at[:, :, groove_start:].add(groove_force.reshape(3, devices, surface))
        accel = (load - internal.reshape(3, devices * own) + contact.reshape(3, devices * own)) / mass[None, :]
        motion = motion + TIMESTEP * accel
        deform = deform + TIMESTEP * motion
    return deform, motion
```

```python
import functools

import jax
import jax.numpy as jnp
from jax import lax
from jax.experimental import pallas as pl
from jax.experimental.pallas import tpu as pltpu
from jax.sharding import PartitionSpec as P

FACE = 1024
WIDTH = 64
LANES = 128
ROWS = 16
PENALTY = 4.0
DASHPOT = 1.0
FRICTION = 2.0
TIMESTEP = 0.25
BF16 = jnp.bfloat16
F32 = jnp.float32
MESH = pl.DeviceIdType.MESH


def parts(x):
    first = x.astype(BF16)
    rest = x - first.astype(F32)
    second = rest.astype(BF16)
    third = (rest - second.astype(F32)).astype(BF16)
    return first, second, third


def one_hot(mask):
    return jnp.where(mask, 1.0, 0.0).astype(BF16)


def dot(a, b):
    return jnp.dot(a, b, preferred_element_type=F32)


def iota(shape, dim):
    return lax.broadcasted_iota(jnp.int32, shape, dim)


def padded_transpose(block):
    rows = block.shape[0]
    return jnp.concatenate([block, jnp.zeros((LANES - rows, LANES), F32)], axis=0).T


def contact_terms(cycle, groove):
    relative = [cycle[k] - groove[k] for k in range(3)]
    intersection = jnp.maximum(relative[0], 0.0)
    closing = cycle[3] - groove[3]
    return [
        intersection * (PENALTY + DASHPOT * closing),
        FRICTION * intersection * relative[1],
        FRICTION * intersection * relative[2],
    ]


def column_of(block, own_blocks, face_blocks):
    upper = own_blocks + face_blocks
    return jnp.where(
        block < face_blocks,
        block + own_blocks,
        jnp.where(block >= upper, block + 2 * face_blocks, block - face_blocks),
    )


def fill_tables(conn_ref, column_ref, pick_ref, back_ref, own_blocks, face_blocks):
    groups = conn_ref.shape[0]
    columns = pick_ref.shape[0]
    for group in range(groups):
        row = column_of(conn_ref[group, 0:1, :] >> 7, own_blocks, face_blocks)
        pick_ref[:, group * LANES : (group + 1) * LANES] = one_hot(iota((columns, LANES), 0) == row)
        col = column_of(column_ref[:, group : group + 1] >> 7, own_blocks, face_blocks)
        back_ref[group * LANES : (group + 1) * LANES, :] = one_hot(iota((LANES, columns), 1) == col)


def gather_tiles(state_ref, pick_ref, tile_ref):
    groups = tile_ref.shape[0]
    for pair in range(groups // 2):
        pick = pick_ref[:, pair * 256 : (pair + 1) * 256]
        found = sum(dot(state_ref[p], pick) for p in range(3))
        tile_ref[2 * pair] = found[:, :LANES]
        tile_ref[2 * pair + 1] = found[:, LANES:]


def element_group(group, stiff_ref, conn_ref, tile_ref, near_ref, spread_ref):
    links = conn_ref[group]
    odd = ((links[0:1, :] >> 6) & 1) == 1
    low = links & 7
    high = (links >> 3) & 7
    for c in range(3):
        tile = jnp.where(
            odd,
            tile_ref[group, c * 128 + 64 : c * 128 + 128, :],
            tile_ref[group, c * 128 : c * 128 + 64, :],
        )
        for j in range(8):
            index = low[j * 8 : j * 8 + 8]
            which = high[j * 8 : j * 8 + 8]
            value = jnp.take_along_axis(tile[0:8], index, axis=0, mode="promise_in_bounds")
            for m in range(1, 8):
                other = jnp.take_along_axis(
                    tile[m * 8 : m * 8 + 8], index, axis=0, mode="promise_in_bounds"
                )
                value = jnp.where(which == m, other, value)
            near_ref[c, j * 8 : j * 8 + 8, :] = value

    def row(i, sums):
        stiff = stiff_ref[group, i]
        hit = iota((WIDTH, LANES), 0) == (conn_ref[group, pl.ds(i, 1), :] & 63)
        out = []
        for c in range(3):
            force = jnp.sum(stiff * near_ref[c], axis=0, keepdims=True)
            out.append(sums[c] + jnp.where(hit, force, 0.0))
        return tuple(out)

    zero = jnp.zeros((WIDTH, LANES), F32)
    sums = lax.fori_loop(0, WIDTH, row, (zero, zero, zero))
    at = pl.ds(pl.multiple_of(group * LANES, LANES), LANES)
    for c in range(3):
        for half in range(2):
            kept = jnp.where(odd if half else jnp.logical_not(odd), sums[c], 0.0)
            for p, part in enumerate(parts(kept)):
                spread_ref[p, c * 128 + half * 64 : c * 128 + half * 64 + 64, at] = part


def kernel(
    counts, disp_in, vel_in, load_ref, mass_ref, stiff_hbm, conn_ref, column_ref, clear_ref,
    target_ref, slot_ref, disp_ref, vel_ref,
    stiff_ref, pick_ref, back_ref, tile_ref, near_ref, spread_ref, state_ref, force_ref, scale_ref,
    pickers, pickers_t, seers, seers_t, note_out, note_in, send_ref, recv_ref,
    face_out, face_in, edge_out, edge_in,
    stiff_sem, note_send, note_recv, block_send, block_recv, face_send, face_recv, edge_send,
    edge_recv,
):
    circ_count, xsec_count, steps, own_blocks, face_blocks = counts
    devices = circ_count * xsec_count
    groups = stiff_ref.shape[0]
    circ, xsec = lax.axis_index("circ"), lax.axis_index("xsec")
    me = circ * xsec_count + xsec
    lower = (lax.rem(circ + circ_count - 1, circ_count), xsec)
    upper = (lax.rem(circ + 1, circ_count), xsec)

    def peer(r):
        other = lax.rem(me + r, devices)
        return other, (other // xsec_count, lax.rem(other, xsec_count))

    copies = [
        pltpu.make_async_copy(
            stiff_hbm.at[:, :, pl.ds(g * LANES, LANES)], stiff_ref.at[g], stiff_sem.at[g]
        )
        for g in range(groups)
    ]
    for copy in copies:
        copy.start()

    barrier = pltpu.get_barrier_semaphore()

    def greet(r, carry):
        pl.semaphore_signal(barrier, inc=1, device_id=peer(r)[1], device_id_type=MESH)
        return carry

    lax.fori_loop(1, devices, greet, 0)

    square = (LANES, LANES)
    note = jnp.zeros(square, F32)
    for s in range(steps):
        dev_row = target_ref[s : s + 1, :]
        dev_square = jnp.broadcast_to(dev_row, square)
        dev_col = dev_square.astype(F32).T.astype(jnp.int32)
        earlier = (dev_col == dev_square) & (iota(square, 0) < iota(square, 1))
        rank_row = jnp.sum(jnp.where(earlier, 1.0, 0.0), axis=0, keepdims=True).astype(jnp.int32)
        code_row = jnp.broadcast_to(dev_row + rank_row * devices, square)
        code_col = code_row.astype(F32).T.astype(jnp.int32)
        for r in range(2):
            mine = code_row == iota(square, 0) + r * devices
            pickers[s, r * LANES : (r + 1) * LANES, :] = one_hot(mine)
            pickers_t[s, :, r * LANES : (r + 1) * LANES] = one_hot(
                code_col == iota(square, 1) + r * devices
            )
            named = jnp.where(mine, (slot_ref[s : s + 1, :] + 1).astype(F32), 0.0)
            named = jnp.sum(named, axis=1, keepdims=True)
            note = note + jnp.where(iota(square, 1) == 2 * s + r, named, 0.0)
    note_out[...] = jnp.zeros(note_out.shape, F32)
    note_out[pl.ds(0, LANES, stride=8), :] = note

    pl.semaphore_wait(barrier, devices - 1)

    def tell(r, carry):
        other, where = peer(r)
        pltpu.make_async_remote_copy(
            src_ref=note_out.at[pl.ds(pl.multiple_of(other * 8, 8), 8)],
            dst_ref=note_in.at[pl.ds(pl.multiple_of(me * 8, 8), 8)],
            send_sem=note_send,
            recv_sem=note_recv,
            device_id=where,
            device_id_type=MESH,
        ).start()
        return carry

    lax.fori_loop(1, devices, tell, 0)
    home = pl.ds(pl.multiple_of(me * 8, 8), 8)
    note_in[home, :] = note_out[home, :]

    for c in range(3):
        disp_ref[c] = disp_in[c]
        vel_ref[c] = vel_in[c]
    scale_ref[...] = TIMESTEP / mass_ref[...]
    fill_tables(conn_ref, column_ref, pick_ref, back_ref, own_blocks, face_blocks)

    told = note_in.at[pl.ds(0, (devices - 1) * 8)]
    pltpu.make_async_copy(told, told, note_recv).wait()
    pltpu.make_async_copy(told, told, note_send).wait()
    heard = note_in[pl.ds(0, LANES, stride=8), :]
    heard_t = heard.T
    for s in range(steps):
        for r in range(2):
            q = 2 * s + r
            seers[s, r * LANES : (r + 1) * LANES, :] = one_hot(
                heard[:, q : q + 1] == (iota(square, 1) + 1).astype(F32)
            )
            seers_t[s, :, r * LANES : (r + 1) * LANES] = one_hot(
                heard_t[q : q + 1, :] == (iota(square, 0) + 1).astype(F32)
            )
    for copy in copies:
        copy.wait()

    surface = LANES
    groove = own_blocks - surface
    lane = iota(square, 1)

    def step(s, carry):
        cycle = [disp_ref[c][:, :surface].T for c in range(3)] + [vel_ref[0][:, :surface].T]
        mate = [disp_ref[c][:, groove:].T for c in range(3)] + [vel_ref[0][:, groove:].T]
        for c in range(3):
            face_out[c * 8 : c * 8 + 8, :] = cycle[c][:8]
            face_out[24 + c * 8 : 24 + c * 8 + 8, :] = mate[c][LANES - 8 :]
        faces = []
        for side, where in ((0, lower), (1, upper)):
            faces.append(
                pltpu.make_async_remote_copy(
                    src_ref=face_out.at[pl.ds(side * 24, 24)],
                    dst_ref=face_in.at[s, pl.ds((1 - side) * 24, 24)],
                    send_sem=face_send.at[s],
                    recv_sem=face_recv.at[s],
                    device_id=where,
                    device_id_type=MESH,
                )
            )
        for copy in faces:
            copy.start()
        mate[0] = mate[0] + clear_ref[...]

        for base, table, data in ((0, pickers, cycle), (8, seers, mate)):
            pieces = parts(jnp.concatenate(data, axis=1))
            packed = sum(dot(table[s], piece) for piece in pieces)
            for r in range(2):
                for k in range(4):
                    send_ref[pl.ds(base + r * 4 + k, LANES, stride=ROWS), :] = packed[
                        r * LANES : (r + 1) * LANES, k * LANES : (k + 1) * LANES
                    ]

        def ship(r, inner):
            other, where = peer(r)
            pltpu.make_async_remote_copy(
                src_ref=send_ref.at[pl.ds(pl.multiple_of(other * ROWS, ROWS), ROWS)],
                dst_ref=recv_ref.at[s, pl.ds(pl.multiple_of(me * ROWS, ROWS), ROWS)],
                send_sem=block_send.at[s],
                recv_sem=block_recv.at[s],
                device_id=where,
                device_id_type=MESH,
            ).start()
            return inner

        lax.fori_loop(1, devices, ship, 0)
        own_rows = pl.ds(pl.multiple_of(me * ROWS, ROWS), ROWS)
        recv_ref[s, own_rows, :] = send_ref[own_rows, :]

        for c in range(3):
            for p, piece in enumerate(parts(disp_ref[c])):
                state_ref[p, c * LANES : (c + 1) * LANES, :own_blocks] = piece
        both = face_in.at[s]
        pltpu.make_async_copy(both, both, face_recv.at[s]).wait()
        halo = padded_transpose(face_in[s])
        for c in range(3):
            turned = pltpu.roll(halo, LANES - 8 * c, 1) if c else halo
            for p, piece in enumerate(parts(turned)):
                state_ref[p, c * LANES : (c + 1) * LANES, own_blocks:] = piece

        gather_tiles(state_ref, pick_ref, tile_ref)

        def group_step(group, inner):
            element_group(group, stiff_ref, conn_ref, tile_ref, near_ref, spread_ref)
            return inner

        lax.fori_loop(0, groups, group_step, 0)
        force_ref[...] = sum(dot(spread_ref[p], back_ref[...]) for p in range(3))

        edge = jnp.zeros(square, F32)
        for c in range(3):
            tail = force_ref[c * LANES : (c + 1) * LANES, own_blocks:]
            turned = pltpu.roll(tail, 8 * c, 1) if c else tail
            here = ((lane >= 8 * c) & (lane < 8 * c + 8)) | (
                (lane >= 24 + 8 * c) & (lane < 32 + 8 * c)
            )
            edge = jnp.where(here, turned, edge)
        edge_out[...] = edge.T[:48]
        for side, where in ((0, lower), (1, upper)):
            pltpu.make_async_remote_copy(
                src_ref=edge_out.at[pl.ds(side * 24, 24)],
                dst_ref=edge_in.at[s, pl.ds((1 - side) * 24, 24)],
                send_sem=edge_send.at[s],
                recv_sem=edge_recv.at[s],
                device_id=where,
                device_id_type=MESH,
            ).start()

        arrived = recv_ref.at[s, pl.ds(0, (devices - 1) * ROWS)]
        pltpu.make_async_copy(arrived, arrived, block_recv.at[s]).wait()

        def rows_of(ref, base, r):
            return [ref[pl.ds(base + r * 4 + k, LANES, stride=ROWS), :] for k in range(4)]

        incoming = recv_ref.at[s]
        on_groove, on_cycle = [], []
        for r in range(2):
            on_groove.append(
                jnp.concatenate(
                    contact_terms(rows_of(incoming, 0, r), rows_of(send_ref, 8, r)), axis=1
                )
            )
            on_cycle.append(
                jnp.concatenate(
                    contact_terms(rows_of(send_ref, 0, r), rows_of(incoming, 8, r)), axis=1
                )
            )
        groove_force = sum(
            dot(seers_t[s], piece) for piece in parts(jnp.concatenate(on_groove, axis=0))
        )
        cycle_force = sum(
            dot(pickers_t[s], piece) for piece in parts(jnp.concatenate(on_cycle, axis=0))
        )

        both = edge_in.at[s]
        pltpu.make_async_copy(both, both, edge_recv.at[s]).wait()
        edge = padded_transpose(edge_in[s])
        for c in range(3):
            span = slice(c * LANES, (c + 1) * LANES)
            first = pltpu.roll(edge, LANES - 8 * c, 1) if c else edge
            last = pltpu.roll(edge, 96 - 8 * c, 1)
            extra = (
                -cycle_force[:, span].T - jnp.where(lane < 8, first, 0.0),
                None,
                groove_force[:, span].T - jnp.where(lane >= LANES - 8, last, 0.0),
            )
            for low, high, add in (
                (0, surface, extra[0]),
                (surface, groove, None),
                (groove, own_blocks, extra[2]),
            ):
                at = slice(low, high)
                pull = load_ref[c][:, at] - force_ref[span, at]
                if add is not None:
                    pull = pull + add
                speed = vel_ref[c, :, at] + pull * scale_ref[:, at]
                vel_ref[c, :, at] = speed
                disp_ref[c, :, at] = disp_ref[c, :, at] + TIMESTEP * speed

        sent = send_ref.at[pl.ds(0, (devices - 1) * ROWS)]
        pltpu.make_async_copy(sent, sent, block_send.at[s]).wait()
        pltpu.make_async_copy(face_out, face_out, face_send.at[s]).wait()
        pltpu.make_async_copy(edge_out, edge_out, edge_send.at[s]).wait()
        return carry

    lax.fori_loop(0, steps, step, 0)


def body(
    displacement, velocity, load, mass, stiffness, connectivity, clearance, match_device, match_slot
):
    steps = match_slot.shape[0]
    circ_count, xsec_count = lax.axis_size("circ"), lax.axis_size("xsec")
    devices = circ_count * xsec_count
    own_blocks = displacement.shape[1] // LANES
    face_blocks = FACE // LANES
    groups = stiffness.shape[2] // LANES
    wide = own_blocks + LANES

    def turned(array):
        return array.reshape(3, own_blocks, LANES).transpose(0, 2, 1)

    links = connectivity.reshape(WIDTH, groups, LANES).transpose(1, 0, 2)
    columns = connectivity[0].reshape(groups, LANES).T
    vm = pl.BlockSpec(memory_space=pltpu.VMEM)
    shape = jax.ShapeDtypeStruct((3, LANES, own_blocks), F32)
    dma = pltpu.SemaphoreType.DMA
    deform, motion = pl.pallas_call(
        functools.partial(kernel, (circ_count, xsec_count, steps, own_blocks, face_blocks)),
        out_shape=(shape, shape),
        in_specs=[vm, vm, vm, vm, pl.BlockSpec(memory_space=pl.ANY), vm, vm, vm, vm, vm],
        out_specs=(vm, vm),
        scratch_shapes=[
            pltpu.VMEM((groups, WIDTH, WIDTH, LANES), F32),
            pltpu.VMEM((wide, groups * LANES), BF16),
            pltpu.VMEM((groups * LANES, wide), BF16),
            pltpu.VMEM((groups, 3 * LANES, LANES), F32),
            pltpu.VMEM((3, WIDTH, LANES), F32),
            pltpu.VMEM((3, 3 * LANES, groups * LANES), BF16),
            pltpu.VMEM((3, 3 * LANES, wide), BF16),
            pltpu.VMEM((3 * LANES, wide), F32),
            pltpu.VMEM((LANES, own_blocks), F32),
            pltpu.VMEM((steps, 2 * LANES, LANES), BF16),
            pltpu.VMEM((steps, LANES, 2 * LANES), BF16),
            pltpu.VMEM((steps, 2 * LANES, LANES), BF16),
            pltpu.VMEM((steps, LANES, 2 * LANES), BF16),
            pltpu.VMEM((devices * 8, LANES), F32),
            pltpu.VMEM((devices * 8, LANES), F32),
            pltpu.VMEM((devices * ROWS, LANES), F32),
            pltpu.VMEM((steps, devices * ROWS, LANES), F32),
            pltpu.VMEM((48, LANES), F32),
            pltpu.VMEM((steps, 48, LANES), F32),
            pltpu.VMEM((48, LANES), F32),
            pltpu.VMEM((steps, 48, LANES), F32),
            dma((groups,)),
            dma,
            dma,
            dma((steps,)),
            dma((steps,)),
            dma((steps,)),
            dma((steps,)),
            dma((steps,)),
            dma((steps,)),
        ],
        compiler_params=pltpu.CompilerParams(
            collective_id=0, has_side_effects=True, vmem_limit_bytes=52 * 2**20
        ),
    )(
        turned(displacement),
        turned(velocity),
        turned(load),
        mass.reshape(own_blocks, LANES).T,
        stiffness,
        links,
        columns,
        clearance,
        match_device[:, :, 0],
        match_slot,
    )

    def restored(array):
        return array.transpose(0, 2, 1).reshape(3, own_blocks * LANES)

    return restored(deform), restored(motion)


def solution(mesh):
    return jax.shard_map(
        body,
        mesh=mesh,
        in_specs=(
            P(None, ("circ", "xsec")),
            P(None, ("circ", "xsec")),
            P(None, ("circ", "xsec")),
            P(("circ", "xsec")),
            P(None, None, ("circ", "xsec")),
            P(None, ("circ", "xsec")),
            P(("circ", "xsec"), None),
            P(None, ("circ", "xsec"), None),
            P(None, ("circ", "xsec")),
        ),
        out_specs=(P(None, ("circ", "xsec")), P(None, ("circ", "xsec"))),
        check_vma=False,
    )
```

```python
import functools

import jax
import jax.numpy as jnp
from jax import lax
from jax.experimental import pallas as pl
from jax.experimental.pallas import tpu as pltpu
from jax.sharding import PartitionSpec as P

FACE = 1024
WIDTH = 64
LANES = 128
ROWS = 16
PENALTY = 4.0
DASHPOT = 1.0
FRICTION = 2.0
TIMESTEP = 0.25
BF16 = jnp.bfloat16
F32 = jnp.float32
MESH = pl.DeviceIdType.MESH


def parts(x):
    first = x.astype(BF16)
    rest = x - first.astype(F32)
    second = rest.astype(BF16)
    third = (rest - second.astype(F32)).astype(BF16)
    return first, second, third


def halves(x):
    first = x.astype(BF16)
    return first, (x - first.astype(F32)).astype(BF16)


def one_hot(mask):
    return jnp.where(mask, 1.0, 0.0).astype(BF16)


def dot(a, b):
    return jnp.dot(a, b, preferred_element_type=F32)


def iota(shape, dim):
    return lax.broadcasted_iota(jnp.int32, shape, dim)


def padded_transpose(block):
    rows = block.shape[0]
    return jnp.concatenate([block, jnp.zeros((LANES - rows, LANES), F32)], axis=0).T


def contact_terms(cycle, groove):
    relative = [cycle[k] - groove[k] for k in range(3)]
    intersection = jnp.maximum(relative[0], 0.0)
    closing = cycle[3] - groove[3]
    return [
        intersection * (PENALTY + DASHPOT * closing),
        FRICTION * intersection * relative[1],
        FRICTION * intersection * relative[2],
    ]


def column_of(block, own_blocks, face_blocks):
    upper = own_blocks + face_blocks
    return jnp.where(
        block < face_blocks,
        block + own_blocks,
        jnp.where(block >= upper, block + 2 * face_blocks, block - face_blocks),
    )


def fill_tables(conn_ref, pick_ref, back_ref, own_blocks, face_blocks):
    groups = conn_ref.shape[1] // LANES
    columns = pick_ref.shape[0]
    for group in range(groups):
        row = column_of(conn_ref[0:1, group * LANES : (group + 1) * LANES] >> 7, own_blocks, face_blocks)
        pick_ref[:, group * LANES : (group + 1) * LANES] = one_hot(iota((columns, LANES), 0) == row)
        col = jnp.broadcast_to(row, (LANES, LANES)).astype(F32).T[:, :1].astype(jnp.int32)
        back_ref[group * LANES : (group + 1) * LANES, :] = one_hot(iota((LANES, columns), 1) == col)


def gather_tiles(state_ref, pick_ref, tile_ref):
    groups = tile_ref.shape[0]
    for pair in range(groups // 2):
        pick = pick_ref[:, pair * 256 : (pair + 1) * 256]
        found = dot(state_ref[0], pick) + dot(state_ref[1], pick)
        tile_ref[2 * pair] = found[:, :LANES]
        tile_ref[2 * pair + 1] = found[:, LANES:]


def element_group(group, stiff_ref, conn_ref, tile_ref, near_ref, spread_ref):
    links = conn_ref[group]
    odd = ((links[0:1, :] >> 6) & 1) == 1
    low = links & 7
    high = (links >> 3) & 7
    for c in range(3):
        tile = jnp.where(
            odd,
            tile_ref[group, c * 128 + 64 : c * 128 + 128, :],
            tile_ref[group, c * 128 : c * 128 + 64, :],
        )
        for j in range(8):
            index = low[j * 8 : j * 8 + 8]
            which = high[j * 8 : j * 8 + 8]
            value = jnp.take_along_axis(tile[0:8], index, axis=0, mode="promise_in_bounds")
            for m in range(1, 8):
                other = jnp.take_along_axis(
                    tile[m * 8 : m * 8 + 8], index, axis=0, mode="promise_in_bounds"
                )
                value = jnp.where(which == m, other, value)
            near_ref[c, j * 8 : j * 8 + 8, :] = value

    def row(i, sums):
        stiff = stiff_ref[group, i]
        hit = iota((WIDTH, LANES), 0) == (conn_ref[group, pl.ds(i, 1), :] & 63)
        out = []
        for c in range(3):
            force = jnp.sum(stiff * near_ref[c], axis=0, keepdims=True)
            out.append(sums[c] + jnp.where(hit, force, 0.0))
        return tuple(out)

    zero = jnp.zeros((WIDTH, LANES), F32)
    sums = lax.fori_loop(0, WIDTH, row, (zero, zero, zero), unroll=8)
    at = pl.ds(pl.multiple_of(group * LANES, LANES), LANES)
    for c in range(3):
        for half in range(2):
            kept = jnp.where(odd if half else jnp.logical_not(odd), sums[c], 0.0)
            for p, part in enumerate(halves(kept)):
                spread_ref[p, c * 128 + half * 64 : c * 128 + half * 64 + 64, at] = part


def kernel(
    counts, disp_in, vel_in, load_in, mass_ref, stiff_hbm, conn_ref, clear_ref,
    target_ref, slot_ref, disp_out, vel_out,
    disp_ref, vel_ref, load_ref, given_ref, link_ref, stiff_ref, pick_ref, back_ref, tile_ref, near_ref, spread_ref, state_ref, force_ref, scale_ref,
    pickers, pickers_t, seers, seers_t, note_out, note_in, send_ref, recv_ref,
    face_out, face_in, edge_out, edge_in,
    given_sem, stiff_sem, note_send, note_recv, block_send, block_recv, face_send, face_recv, edge_send,
    edge_recv,
):
    circ_count, xsec_count, steps, own_blocks, face_blocks = counts
    devices = circ_count * xsec_count
    groups = stiff_ref.shape[0]
    circ, xsec = lax.axis_index("circ"), lax.axis_index("xsec")
    me = circ * xsec_count + xsec
    lower = (lax.rem(circ + circ_count - 1, circ_count), xsec)
    upper = (lax.rem(circ + 1, circ_count), xsec)

    def peer(r):
        other = lax.rem(me + r, devices)
        return other, (other // xsec_count, lax.rem(other, xsec_count))

    given = [
        pltpu.make_async_copy(source, given_ref.at[i], given_sem.at[i])
        for i, source in enumerate((disp_in, vel_in, load_in))
    ]
    for copy in given:
        copy.start()
    copies = [
        pltpu.make_async_copy(
            stiff_hbm.at[:, :, pl.ds(g * LANES, LANES)], stiff_ref.at[g], stiff_sem.at[g]
        )
        for g in range(groups)
    ]
    for copy in copies:
        copy.start()

    barrier = pltpu.get_barrier_semaphore()

    def greet(r, carry):
        pl.semaphore_signal(barrier, inc=1, device_id=peer(r)[1], device_id_type=MESH)
        return carry

    lax.fori_loop(1, devices, greet, 0)

    square = (LANES, LANES)
    note = jnp.zeros(square, F32)
    for s in range(steps):
        dev_row = target_ref[s]
        dev_square = jnp.broadcast_to(dev_row, square)
        dev_col = dev_square.astype(F32).T.astype(jnp.int32)
        earlier = (dev_col == dev_square) & (iota(square, 0) < iota(square, 1))
        rank_row = jnp.sum(jnp.where(earlier, 1.0, 0.0), axis=0, keepdims=True).astype(jnp.int32)
        code_row = jnp.broadcast_to(dev_row + rank_row * devices, square)
        code_col = code_row.astype(F32).T.astype(jnp.int32)
        for r in range(2):
            mine = code_row == iota(square, 0) + r * devices
            pickers[s, r * LANES : (r + 1) * LANES, :] = one_hot(mine)
            pickers_t[s, :, r * LANES : (r + 1) * LANES] = one_hot(
                code_col == iota(square, 1) + r * devices
            )
            named = jnp.where(mine, (slot_ref[s : s + 1, :] + 1).astype(F32), 0.0)
            named = jnp.sum(named, axis=1, keepdims=True)
            note = note + jnp.where(iota(square, 1) == 2 * s + r, named, 0.0)
    note_out[...] = jnp.zeros(note_out.shape, F32)
    note_out[pl.ds(0, LANES, stride=8), :] = note

    for i, ref in enumerate((disp_ref, vel_ref, load_ref)):
        given[i].wait()
        for c in range(3):
            ref[c] = given_ref[i, :, c, :].T
    scale_ref[...] = TIMESTEP / mass_ref[...].T

    pl.semaphore_wait(barrier, devices - 1)

    def tell(r, carry):
        other, where = peer(r)
        pltpu.make_async_remote_copy(
            src_ref=note_out.at[pl.ds(pl.multiple_of(other * 8, 8), 8)],
            dst_ref=note_in.at[pl.ds(pl.multiple_of(me * 8, 8), 8)],
            send_sem=note_send,
            recv_sem=note_recv,
            device_id=where,
            device_id_type=MESH,
        ).start()
        return carry

    lax.fori_loop(1, devices, tell, 0)
    home = pl.ds(pl.multiple_of(me * 8, 8), 8)
    note_in[home, :] = note_out[home, :]

    for group in range(groups):
        link_ref[group] = conn_ref[:, group * LANES : (group + 1) * LANES]
    fill_tables(conn_ref, pick_ref, back_ref, own_blocks, face_blocks)

    told = note_in.at[pl.ds(0, (devices - 1) * 8)]
    pltpu.make_async_copy(told, told, note_recv).wait()
    pltpu.make_async_copy(told, told, note_send).wait()
    heard = note_in[pl.ds(0, LANES, stride=8), :]
    heard_t = heard.T
    for s in range(steps):
        for r in range(2):
            q = 2 * s + r
            seers[s, r * LANES : (r + 1) * LANES, :] = one_hot(
                heard[:, q : q + 1] == (iota(square, 1) + 1).astype(F32)
            )
            seers_t[s, :, r * LANES : (r + 1) * LANES] = one_hot(
                heard_t[q : q + 1, :] == (iota(square, 0) + 1).astype(F32)
            )
    for copy in copies:
        copy.wait()

    surface = LANES
    groove = own_blocks - surface
    lane = iota(square, 1)

    def step(s, carry):
        cycle = [disp_ref[c][:, :surface].T for c in range(3)] + [vel_ref[0][:, :surface].T]
        mate = [disp_ref[c][:, groove:].T for c in range(3)] + [vel_ref[0][:, groove:].T]
        for c in range(3):
            face_out[c * 8 : c * 8 + 8, :] = cycle[c][:8]
            face_out[24 + c * 8 : 24 + c * 8 + 8, :] = mate[c][LANES - 8 :]
        faces = []
        for side, where in ((0, lower), (1, upper)):
            faces.append(
                pltpu.make_async_remote_copy(
                    src_ref=face_out.at[pl.ds(side * 24, 24)],
                    dst_ref=face_in.at[s, pl.ds((1 - side) * 24, 24)],
                    send_sem=face_send.at[s],
                    recv_sem=face_recv.at[s],
                    device_id=where,
                    device_id_type=MESH,
                )
            )
        for copy in faces:
            copy.start()
        mate[0] = mate[0] + clear_ref[...]

        for base, table, data in ((0, pickers, cycle), (8, seers, mate)):
            pieces = parts(jnp.concatenate(data, axis=1))
            packed = sum(dot(table[s], piece) for piece in pieces)
            for r in range(2):
                for k in range(4):
                    send_ref[pl.ds(base + r * 4 + k, LANES, stride=ROWS), :] = packed[
                        r * LANES : (r + 1) * LANES, k * LANES : (k + 1) * LANES
                    ]

        def ship(r, inner):
            other, where = peer(r)
            pltpu.make_async_remote_copy(
                src_ref=send_ref.at[pl.ds(pl.multiple_of(other * ROWS, ROWS), ROWS)],
                dst_ref=recv_ref.at[s, pl.ds(pl.multiple_of(me * ROWS, ROWS), ROWS)],
                send_sem=block_send.at[s],
                recv_sem=block_recv.at[s],
                device_id=where,
                device_id_type=MESH,
            ).start()
            return inner

        lax.fori_loop(1, devices, ship, 0)
        own_rows = pl.ds(pl.multiple_of(me * ROWS, ROWS), ROWS)
        recv_ref[s, own_rows, :] = send_ref[own_rows, :]

        for c in range(3):
            for p, piece in enumerate(halves(disp_ref[c])):
                state_ref[p, c * LANES : (c + 1) * LANES, :own_blocks] = piece
        both = face_in.at[s]
        pltpu.make_async_copy(both, both, face_recv.at[s]).wait()
        halo = padded_transpose(face_in[s])
        for c in range(3):
            turned = pltpu.roll(halo, LANES - 8 * c, 1) if c else halo
            for p, piece in enumerate(halves(turned)):
                state_ref[p, c * LANES : (c + 1) * LANES, own_blocks:] = piece

        gather_tiles(state_ref, pick_ref, tile_ref)

        def group_step(group, inner):
            element_group(group, stiff_ref, link_ref, tile_ref, near_ref, spread_ref)
            return inner

        lax.fori_loop(0, groups, group_step, 0)
        tails = dot(spread_ref[0], back_ref[:, own_blocks:]) + dot(
            spread_ref[1], back_ref[:, own_blocks:]
        )

        edge = jnp.zeros(square, F32)
        for c in range(3):
            tail = tails[c * LANES : (c + 1) * LANES]
            turned = pltpu.roll(tail, 8 * c, 1) if c else tail
            here = ((lane >= 8 * c) & (lane < 8 * c + 8)) | (
                (lane >= 24 + 8 * c) & (lane < 32 + 8 * c)
            )
            edge = jnp.where(here, turned, edge)
        edge_out[...] = edge.T[:48]
        for side, where in ((0, lower), (1, upper)):
            pltpu.make_async_remote_copy(
                src_ref=edge_out.at[pl.ds(side * 24, 24)],
                dst_ref=edge_in.at[s, pl.ds((1 - side) * 24, 24)],
                send_sem=edge_send.at[s],
                recv_sem=edge_recv.at[s],
                device_id=where,
                device_id_type=MESH,
            ).start()

        force_ref[...] = dot(spread_ref[0], back_ref[:, :own_blocks]) + dot(
            spread_ref[1], back_ref[:, :own_blocks]
        )
        arrived = recv_ref.at[s, pl.ds(0, (devices - 1) * ROWS)]
        pltpu.make_async_copy(arrived, arrived, block_recv.at[s]).wait()

        def rows_of(ref, base, r):
            return [ref[pl.ds(base + r * 4 + k, LANES, stride=ROWS), :] for k in range(4)]

        incoming = recv_ref.at[s]
        on_groove, on_cycle = [], []
        for r in range(2):
            on_groove.append(
                jnp.concatenate(
                    contact_terms(rows_of(incoming, 0, r), rows_of(send_ref, 8, r)), axis=1
                )
            )
            on_cycle.append(
                jnp.concatenate(
                    contact_terms(rows_of(send_ref, 0, r), rows_of(incoming, 8, r)), axis=1
                )
            )
        groove_force = sum(
            dot(seers_t[s], piece) for piece in parts(jnp.concatenate(on_groove, axis=0))
        )
        cycle_force = sum(
            dot(pickers_t[s], piece) for piece in parts(jnp.concatenate(on_cycle, axis=0))
        )

        both = edge_in.at[s]
        pltpu.make_async_copy(both, both, edge_recv.at[s]).wait()
        edge = padded_transpose(edge_in[s])
        for c in range(3):
            span = slice(c * LANES, (c + 1) * LANES)
            first = pltpu.roll(edge, LANES - 8 * c, 1) if c else edge
            last = pltpu.roll(edge, 96 - 8 * c, 1)
            extra = (
                -cycle_force[:, span].T - jnp.where(lane < 8, first, 0.0),
                None,
                groove_force[:, span].T - jnp.where(lane >= LANES - 8, last, 0.0),
            )
            for low, high, add in (
                (0, surface, extra[0]),
                (surface, groove, None),
                (groove, own_blocks, extra[2]),
            ):
                at = slice(low, high)
                pull = load_ref[c][:, at] - force_ref[span, at]
                if add is not None:
                    pull = pull + add
                speed = vel_ref[c, :, at] + pull * scale_ref[:, at]
                vel_ref[c, :, at] = speed
                disp_ref[c, :, at] = disp_ref[c, :, at] + TIMESTEP * speed

        sent = send_ref.at[pl.ds(0, (devices - 1) * ROWS)]
        pltpu.make_async_copy(sent, sent, block_send.at[s]).wait()
        pltpu.make_async_copy(face_out, face_out, face_send.at[s]).wait()
        pltpu.make_async_copy(edge_out, edge_out, edge_send.at[s]).wait()
        return carry

    lax.fori_loop(0, steps, step, 0)
    for c in range(3):
        disp_out[:, c, :] = disp_ref[c].T
        vel_out[:, c, :] = vel_ref[c].T


def body(
    displacement, velocity, load, mass, stiffness, connectivity, clearance, match_device, match_slot
):
    steps = match_slot.shape[0]
    circ_count, xsec_count = lax.axis_size("circ"), lax.axis_size("xsec")
    devices = circ_count * xsec_count
    own_blocks = displacement.shape[1] // LANES
    face_blocks = FACE // LANES
    groups = stiffness.shape[2] // LANES
    wide = own_blocks + LANES

    def turned(array):
        return array.reshape(3, own_blocks, LANES).transpose(1, 0, 2)

    vm = pl.BlockSpec(memory_space=pltpu.VMEM)
    far = pl.BlockSpec(memory_space=pl.ANY)
    shape = jax.ShapeDtypeStruct((own_blocks, 3, LANES), F32)
    dma = pltpu.SemaphoreType.DMA
    deform, motion = pl.pallas_call(
        functools.partial(kernel, (circ_count, xsec_count, steps, own_blocks, face_blocks)),
        out_shape=(shape, shape),
        in_specs=[far, far, far, vm, far, vm, vm, vm, vm],
        out_specs=(vm, vm),
        scratch_shapes=[
            pltpu.VMEM((3, LANES, own_blocks), F32),
            pltpu.VMEM((3, LANES, own_blocks), F32),
            pltpu.VMEM((3, LANES, own_blocks), F32),
            pltpu.VMEM((3, own_blocks, 3, LANES), F32),
            pltpu.VMEM((groups, WIDTH, LANES), jnp.int32),
            pltpu.VMEM((groups, WIDTH, WIDTH, LANES), F32),
            pltpu.VMEM((wide, groups * LANES), BF16),
            pltpu.VMEM((groups * LANES, wide), BF16),
            pltpu.VMEM((groups, 3 * LANES, LANES), F32),
            pltpu.VMEM((3, WIDTH, LANES), F32),
            pltpu.VMEM((2, 3 * LANES, groups * LANES), BF16),
            pltpu.VMEM((2, 3 * LANES, wide), BF16),
            pltpu.VMEM((3 * LANES, own_blocks), F32),
            pltpu.VMEM((LANES, own_blocks), F32),
            pltpu.VMEM((steps, 2 * LANES, LANES), BF16),
            pltpu.VMEM((steps, LANES, 2 * LANES), BF16),
            pltpu.VMEM((steps, 2 * LANES, LANES), BF16),
            pltpu.VMEM((steps, LANES, 2 * LANES), BF16),
            pltpu.VMEM((devices * 8, LANES), F32),
            pltpu.VMEM((devices * 8, LANES), F32),
            pltpu.VMEM((devices * ROWS, LANES), F32),
            pltpu.VMEM((steps, devices * ROWS, LANES), F32),
            pltpu.VMEM((48, LANES), F32),
            pltpu.VMEM((steps, 48, LANES), F32),
            pltpu.VMEM((48, LANES), F32),
            pltpu.VMEM((steps, 48, LANES), F32),
            dma((3,)),
            dma((groups,)),
            dma,
            dma,
            dma((steps,)),
            dma((steps,)),
            dma((steps,)),
            dma((steps,)),
            dma((steps,)),
            dma((steps,)),
        ],
        compiler_params=pltpu.CompilerParams(
            collective_id=0, has_side_effects=True, vmem_limit_bytes=62 * 2**20
        ),
    )(
        turned(displacement),
        turned(velocity),
        turned(load),
        mass.reshape(own_blocks, LANES),
        stiffness,
        connectivity,
        clearance,
        match_device.transpose(0, 2, 1),
        match_slot,
    )

    def restored(array):
        return array.transpose(1, 0, 2).reshape(3, own_blocks * LANES)

    return restored(deform), restored(motion)


def solution(mesh):
    return jax.shard_map(
        body,
        mesh=mesh,
        in_specs=(
            P(None, ("circ", "xsec")),
            P(None, ("circ", "xsec")),
            P(None, ("circ", "xsec")),
            P(("circ", "xsec")),
            P(None, None, ("circ", "xsec")),
            P(None, ("circ", "xsec")),
            P(("circ", "xsec"), None),
            P(None, ("circ", "xsec"), None),
            P(None, ("circ", "xsec")),
        ),
        out_specs=(P(None, ("circ", "xsec")), P(None, ("circ", "xsec"))),
        check_vma=False,
    )
```

```python
import functools

import jax
import jax.numpy as jnp
from jax import lax
from jax.experimental import pallas as pl
from jax.experimental.pallas import tpu as pltpu
from jax.sharding import PartitionSpec as P

FACE = 1024
WIDTH = 64
LANES = 128
ROWS = 16
PENALTY = 4.0
DASHPOT = 1.0
FRICTION = 2.0
TIMESTEP = 0.25
BF16 = jnp.bfloat16
F32 = jnp.float32
MESH = pl.DeviceIdType.MESH


def parts(x):
    first = x.astype(BF16)
    rest = x - first.astype(F32)
    second = rest.astype(BF16)
    third = (rest - second.astype(F32)).astype(BF16)
    return first, second, third


def halves(x):
    first = x.astype(BF16)
    return first, (x - first.astype(F32)).astype(BF16)


def one_hot(mask):
    return jnp.where(mask, 1.0, 0.0).astype(BF16)


def dot(a, b):
    return jnp.dot(a, b, preferred_element_type=F32)


def iota(shape, dim):
    return lax.broadcasted_iota(jnp.int32, shape, dim)


def padded_transpose(block):
    rows = block.shape[0]
    return jnp.concatenate([block, jnp.zeros((LANES - rows, LANES), F32)], axis=0).T


def contact_terms(cycle, groove):
    relative = [cycle[k] - groove[k] for k in range(3)]
    intersection = jnp.maximum(relative[0], 0.0)
    closing = cycle[3] - groove[3]
    return [
        intersection * (PENALTY + DASHPOT * closing),
        FRICTION * intersection * relative[1],
        FRICTION * intersection * relative[2],
    ]


def column_of(block, own_blocks, face_blocks):
    upper = own_blocks + face_blocks
    return jnp.where(
        block < face_blocks,
        block + own_blocks,
        jnp.where(block >= upper, block + 2 * face_blocks, block - face_blocks),
    )


def fill_tables(conn_ref, pick_ref, back_ref, own_blocks, face_blocks):
    groups = conn_ref.shape[1] // LANES
    columns = pick_ref.shape[0]
    for group in range(groups):
        row = column_of(conn_ref[0:1, group * LANES : (group + 1) * LANES] >> 7, own_blocks, face_blocks)
        pick_ref[:, group * LANES : (group + 1) * LANES] = one_hot(iota((columns, LANES), 0) == row)
        col = jnp.broadcast_to(row, (LANES, LANES)).astype(F32).T[:, :1].astype(jnp.int32)
        back_ref[group * LANES : (group + 1) * LANES, :] = one_hot(iota((LANES, columns), 1) == col)


def gather_tiles(state_ref, pick_ref, tile_ref):
    groups = tile_ref.shape[0]
    for pair in range(groups // 2):
        pick = pick_ref[:, pair * 256 : (pair + 1) * 256]
        found = dot(state_ref[0], pick) + dot(state_ref[1], pick)
        tile_ref[2 * pair] = found[:, :LANES]
        tile_ref[2 * pair + 1] = found[:, LANES:]


def pick_rows(table, index):
    out = []
    for j in range(0, WIDTH, 8):
        low = index[j : j + 8] & 7
        high = index[j : j + 8] >> 3
        value = jnp.take_along_axis(table[0:8], low, axis=0, mode="promise_in_bounds")
        for m in range(1, WIDTH // 8):
            other = jnp.take_along_axis(
                table[m * 8 : m * 8 + 8], low, axis=0, mode="promise_in_bounds"
            )
            value = jnp.where(high == m, other, value)
        out.append(value)
    return jnp.concatenate(out, axis=0)


def running_sums(rows):
    at = iota((8, LANES), 0)
    base = jnp.zeros((1, LANES), F32)
    out = []
    for j in range(0, WIDTH, 8):
        piece = rows[j : j + 8]
        for by in (1, 2, 4):
            piece = piece + jnp.where(at >= by, pltpu.roll(piece, by, 0), 0.0)
        piece = piece + base
        base = piece[7:8]
        out.append(piece)
    return jnp.concatenate(out, axis=0)


def sort_links(group, link_ref, key_ref, order_ref, end_ref):
    at = iota((WIDTH, LANES), 0)
    local = link_ref[group] & 63
    keys = local * WIDTH + at
    key_ref[...] = keys

    def count(i, carry):
        place, end = carry
        key = key_ref[pl.ds(i, 1), :]
        place = place + jnp.where(key < keys, 1, 0)
        end = end + jnp.where(key < (at + 1) * WIDTH, 1, 0)
        return place, end

    zero = jnp.zeros((WIDTH, LANES), jnp.int32)
    place, end = lax.fori_loop(0, WIDTH, count, (zero, zero), unroll=4)
    end_ref[group] = end
    key_ref[...] = place

    def invert(i, order):
        return jnp.where(key_ref[pl.ds(i, 1), :] == at, i, order)

    order_ref[group] = lax.fori_loop(0, WIDTH, invert, zero, unroll=4)


def element_group(group, stiff_ref, link_ref, order_ref, end_ref, tile_ref, row_ref, spread_ref):
    links = link_ref[group]
    odd = ((links[0:1, :] >> 6) & 1) == 1
    local = links & 63
    near = []
    for c in range(3):
        tile = jnp.where(
            odd,
            tile_ref[group, c * 128 + 64 : c * 128 + 128, :],
            tile_ref[group, c * 128 : c * 128 + 64, :],
        )
        near.append(pick_rows(tile, local))

    def row(i, carry):
        stiff = stiff_ref[group, i]
        for c in range(3):
            row_ref[c, pl.ds(i, 1), :] = jnp.sum(stiff * near[c], axis=0, keepdims=True)
        return carry

    lax.fori_loop(0, WIDTH, row, 0, unroll=8)
    order = order_ref[group]
    end = end_ref[group]
    last = jnp.maximum(end - 1, 0)
    at = pl.ds(pl.multiple_of(group * LANES, LANES), LANES)
    for c in range(3):
        totals = pick_rows(running_sums(pick_rows(row_ref[c], order)), last)
        totals = jnp.where(end > 0, totals, 0.0)
        before = jnp.where(iota((WIDTH, LANES), 0) > 0, pltpu.roll(totals, 1, 0), 0.0)
        sums = totals - before
        for half in range(2):
            kept = jnp.where(odd if half else jnp.logical_not(odd), sums, 0.0)
            for p, part in enumerate(halves(kept)):
                spread_ref[p, c * 128 + half * 64 : c * 128 + half * 64 + 64, at] = part


def kernel(
    counts, disp_in, vel_in, load_in, mass_ref, stiff_hbm, conn_ref, clear_ref,
    target_ref, slot_ref, disp_out, vel_out,
    disp_ref, vel_ref, load_ref, given_ref, key_ref, order_ref, end_ref, link_ref, stiff_ref, pick_ref, back_ref, tile_ref, near_ref, spread_ref, state_ref, force_ref, scale_ref,
    pickers, pickers_t, seers, seers_t, note_out, note_in, send_ref, recv_ref,
    face_out, face_in, edge_out, edge_in,
    given_sem, stiff_sem, note_send, note_recv, block_send, block_recv, face_send, face_recv, edge_send,
    edge_recv,
):
    circ_count, xsec_count, steps, own_blocks, face_blocks = counts
    devices = circ_count * xsec_count
    groups = stiff_ref.shape[0]
    circ, xsec = lax.axis_index("circ"), lax.axis_index("xsec")
    me = circ * xsec_count + xsec
    lower = (lax.rem(circ + circ_count - 1, circ_count), xsec)
    upper = (lax.rem(circ + 1, circ_count), xsec)

    def peer(r):
        other = lax.rem(me + r, devices)
        return other, (other // xsec_count, lax.rem(other, xsec_count))

    given = [
        pltpu.make_async_copy(source, given_ref.at[i], given_sem.at[i])
        for i, source in enumerate((disp_in, vel_in, load_in))
    ]
    for copy in given:
        copy.start()
    copies = [
        pltpu.make_async_copy(
            stiff_hbm.at[:, :, pl.ds(g * LANES, LANES)], stiff_ref.at[g], stiff_sem.at[g]
        )
        for g in range(groups)
    ]
    for copy in copies:
        copy.start()

    barrier = pltpu.get_barrier_semaphore()

    def greet(r, carry):
        pl.semaphore_signal(barrier, inc=1, device_id=peer(r)[1], device_id_type=MESH)
        return carry

    lax.fori_loop(1, devices, greet, 0)

    square = (LANES, LANES)
    note = jnp.zeros(square, F32)
    for s in range(steps):
        dev_row = target_ref[s]
        dev_square = jnp.broadcast_to(dev_row, square)
        dev_col = dev_square.astype(F32).T.astype(jnp.int32)
        earlier = (dev_col == dev_square) & (iota(square, 0) < iota(square, 1))
        rank_row = jnp.sum(jnp.where(earlier, 1.0, 0.0), axis=0, keepdims=True).astype(jnp.int32)
        code_row = jnp.broadcast_to(dev_row + rank_row * devices, square)
        code_col = code_row.astype(F32).T.astype(jnp.int32)
        for r in range(2):
            mine = code_row == iota(square, 0) + r * devices
            pickers[s, r * LANES : (r + 1) * LANES, :] = one_hot(mine)
            pickers_t[s, :, r * LANES : (r + 1) * LANES] = one_hot(
                code_col == iota(square, 1) + r * devices
            )
            named = jnp.where(mine, (slot_ref[s : s + 1, :] + 1).astype(F32), 0.0)
            named = jnp.sum(named, axis=1, keepdims=True)
            note = note + jnp.where(iota(square, 1) == 2 * s + r, named, 0.0)
    note_out[...] = jnp.zeros(note_out.shape, F32)
    note_out[pl.ds(0, LANES, stride=8), :] = note

    for i, ref in enumerate((disp_ref, vel_ref, load_ref)):
        given[i].wait()
        for c in range(3):
            ref[c] = given_ref[i, :, c, :].T
    scale_ref[...] = TIMESTEP / mass_ref[...].T

    pl.semaphore_wait(barrier, devices - 1)

    def tell(r, carry):
        other, where = peer(r)
        pltpu.make_async_remote_copy(
            src_ref=note_out.at[pl.ds(pl.multiple_of(other * 8, 8), 8)],
            dst_ref=note_in.at[pl.ds(pl.multiple_of(me * 8, 8), 8)],
            send_sem=note_send,
            recv_sem=note_recv,
            device_id=where,
            device_id_type=MESH,
        ).start()
        return carry

    lax.fori_loop(1, devices, tell, 0)
    home = pl.ds(pl.multiple_of(me * 8, 8), 8)
    note_in[home, :] = note_out[home, :]

    for group in range(groups):
        link_ref[group] = conn_ref[:, group * LANES : (group + 1) * LANES]
    fill_tables(conn_ref, pick_ref, back_ref, own_blocks, face_blocks)

    def sort_step(group, carry):
        sort_links(group, link_ref, key_ref, order_ref, end_ref)
        return carry

    lax.fori_loop(0, groups, sort_step, 0)

    told = note_in.at[pl.ds(0, (devices - 1) * 8)]
    pltpu.make_async_copy(told, told, note_recv).wait()
    pltpu.make_async_copy(told, told, note_send).wait()
    heard = note_in[pl.ds(0, LANES, stride=8), :]
    heard_t = heard.T
    for s in range(steps):
        for r in range(2):
            q = 2 * s + r
            seers[s, r * LANES : (r + 1) * LANES, :] = one_hot(
                heard[:, q : q + 1] == (iota(square, 1) + 1).astype(F32)
            )
            seers_t[s, :, r * LANES : (r + 1) * LANES] = one_hot(
                heard_t[q : q + 1, :] == (iota(square, 0) + 1).astype(F32)
            )
    for copy in copies:
        copy.wait()

    surface = LANES
    groove = own_blocks - surface
    lane = iota(square, 1)

    def step(s, carry):
        cycle = [disp_ref[c][:, :surface].T for c in range(3)] + [vel_ref[0][:, :surface].T]
        mate = [disp_ref[c][:, groove:].T for c in range(3)] + [vel_ref[0][:, groove:].T]
        for c in range(3):
            face_out[c * 8 : c * 8 + 8, :] = cycle[c][:8]
            face_out[24 + c * 8 : 24 + c * 8 + 8, :] = mate[c][LANES - 8 :]
        faces = []
        for side, where in ((0, lower), (1, upper)):
            faces.append(
                pltpu.make_async_remote_copy(
                    src_ref=face_out.at[pl.ds(side * 24, 24)],
                    dst_ref=face_in.at[s, pl.ds((1 - side) * 24, 24)],
                    send_sem=face_send.at[s],
                    recv_sem=face_recv.at[s],
                    device_id=where,
                    device_id_type=MESH,
                )
            )
        for copy in faces:
            copy.start()
        mate[0] = mate[0] + clear_ref[...]

        for base, table, data in ((0, pickers, cycle), (8, seers, mate)):
            pieces = parts(jnp.concatenate(data, axis=1))
            packed = sum(dot(table[s], piece) for piece in pieces)
            for r in range(2):
                for k in range(4):
                    send_ref[pl.ds(base + r * 4 + k, LANES, stride=ROWS), :] = packed[
                        r * LANES : (r + 1) * LANES, k * LANES : (k + 1) * LANES
                    ]

        def ship(r, inner):
            other, where = peer(r)
            pltpu.make_async_remote_copy(
                src_ref=send_ref.at[pl.ds(pl.multiple_of(other * ROWS, ROWS), ROWS)],
                dst_ref=recv_ref.at[s, pl.ds(pl.multiple_of(me * ROWS, ROWS), ROWS)],
                send_sem=block_send.at[s],
                recv_sem=block_recv.at[s],
                device_id=where,
                device_id_type=MESH,
            ).start()
            return inner

        lax.fori_loop(1, devices, ship, 0)
        own_rows = pl.ds(pl.multiple_of(me * ROWS, ROWS), ROWS)
        recv_ref[s, own_rows, :] = send_ref[own_rows, :]

        for c in range(3):
            for p, piece in enumerate(halves(disp_ref[c])):
                state_ref[p, c * LANES : (c + 1) * LANES, :own_blocks] = piece
        both = face_in.at[s]
        pltpu.make_async_copy(both, both, face_recv.at[s]).wait()
        halo = padded_transpose(face_in[s])
        for c in range(3):
            turned = pltpu.roll(halo, LANES - 8 * c, 1) if c else halo
            for p, piece in enumerate(halves(turned)):
                state_ref[p, c * LANES : (c + 1) * LANES, own_blocks:] = piece

        gather_tiles(state_ref, pick_ref, tile_ref)

        def group_step(group, inner):
            element_group(
                group, stiff_ref, link_ref, order_ref, end_ref, tile_ref, near_ref, spread_ref
            )
            return inner

        lax.fori_loop(0, groups, group_step, 0)
        tails = dot(spread_ref[0], back_ref[:, own_blocks:]) + dot(
            spread_ref[1], back_ref[:, own_blocks:]
        )

        edge = jnp.zeros(square, F32)
        for c in range(3):
            tail = tails[c * LANES : (c + 1) * LANES]
            turned = pltpu.roll(tail, 8 * c, 1) if c else tail
            here = ((lane >= 8 * c) & (lane < 8 * c + 8)) | (
                (lane >= 24 + 8 * c) & (lane < 32 + 8 * c)
            )
            edge = jnp.where(here, turned, edge)
        edge_out[...] = edge.T[:48]
        for side, where in ((0, lower), (1, upper)):
            pltpu.make_async_remote_copy(
                src_ref=edge_out.at[pl.ds(side * 24, 24)],
                dst_ref=edge_in.at[s, pl.ds((1 - side) * 24, 24)],
                send_sem=edge_send.at[s],
                recv_sem=edge_recv.at[s],
                device_id=where,
                device_id_type=MESH,
            ).start()

        force_ref[...] = dot(spread_ref[0], back_ref[:, :own_blocks]) + dot(
            spread_ref[1], back_ref[:, :own_blocks]
        )
        arrived = recv_ref.at[s, pl.ds(0, (devices - 1) * ROWS)]
        pltpu.make_async_copy(arrived, arrived, block_recv.at[s]).wait()

        def rows_of(ref, base, r):
            return [ref[pl.ds(base + r * 4 + k, LANES, stride=ROWS), :] for k in range(4)]

        incoming = recv_ref.at[s]
        on_groove, on_cycle = [], []
        for r in range(2):
            on_groove.append(
                jnp.concatenate(
                    contact_terms(rows_of(incoming, 0, r), rows_of(send_ref, 8, r)), axis=1
                )
            )
            on_cycle.append(
                jnp.concatenate(
                    contact_terms(rows_of(send_ref, 0, r), rows_of(incoming, 8, r)), axis=1
                )
            )
        groove_force = sum(
            dot(seers_t[s], piece) for piece in parts(jnp.concatenate(on_groove, axis=0))
        )
        cycle_force = sum(
            dot(pickers_t[s], piece) for piece in parts(jnp.concatenate(on_cycle, axis=0))
        )

        both = edge_in.at[s]
        pltpu.make_async_copy(both, both, edge_recv.at[s]).wait()
        edge = padded_transpose(edge_in[s])
        for c in range(3):
            span = slice(c * LANES, (c + 1) * LANES)
            first = pltpu.roll(edge, LANES - 8 * c, 1) if c else edge
            last = pltpu.roll(edge, 96 - 8 * c, 1)
            extra = (
                -cycle_force[:, span].T - jnp.where(lane < 8, first, 0.0),
                None,
                groove_force[:, span].T - jnp.where(lane >= LANES - 8, last, 0.0),
            )
            for low, high, add in (
                (0, surface, extra[0]),
                (surface, groove, None),
                (groove, own_blocks, extra[2]),
            ):
                at = slice(low, high)
                pull = load_ref[c][:, at] - force_ref[span, at]
                if add is not None:
                    pull = pull + add
                speed = vel_ref[c, :, at] + pull * scale_ref[:, at]
                vel_ref[c, :, at] = speed
                disp_ref[c, :, at] = disp_ref[c, :, at] + TIMESTEP * speed

        sent = send_ref.at[pl.ds(0, (devices - 1) * ROWS)]
        pltpu.make_async_copy(sent, sent, block_send.at[s]).wait()
        pltpu.make_async_copy(face_out, face_out, face_send.at[s]).wait()
        pltpu.make_async_copy(edge_out, edge_out, edge_send.at[s]).wait()
        return carry

    lax.fori_loop(0, steps, step, 0)
    for c in range(3):
        given_ref[0, :, c, :] = disp_ref[c].T
        given_ref[1, :, c, :] = vel_ref[c].T
    back = [
        pltpu.make_async_copy(given_ref.at[i], out, given_sem.at[i])
        for i, out in enumerate((disp_out, vel_out))
    ]
    for copy in back:
        copy.start()
    for copy in back:
        copy.wait()


def body(
    displacement, velocity, load, mass, stiffness, connectivity, clearance, match_device, match_slot
):
    steps = match_slot.shape[0]
    circ_count, xsec_count = lax.axis_size("circ"), lax.axis_size("xsec")
    devices = circ_count * xsec_count
    own_blocks = displacement.shape[1] // LANES
    face_blocks = FACE // LANES
    groups = stiffness.shape[2] // LANES
    wide = own_blocks + LANES

    def turned(array):
        return array.reshape(3, own_blocks, LANES).transpose(1, 0, 2)

    vm = pl.BlockSpec(memory_space=pltpu.VMEM)
    far = pl.BlockSpec(memory_space=pl.ANY)
    shape = jax.ShapeDtypeStruct((own_blocks, 3, LANES), F32)
    dma = pltpu.SemaphoreType.DMA
    deform, motion = pl.pallas_call(
        functools.partial(kernel, (circ_count, xsec_count, steps, own_blocks, face_blocks)),
        out_shape=(shape, shape),
        in_specs=[far, far, far, vm, far, vm, vm, vm, vm],
        out_specs=(far, far),
        scratch_shapes=[
            pltpu.VMEM((3, LANES, own_blocks), F32),
            pltpu.VMEM((3, LANES, own_blocks), F32),
            pltpu.VMEM((3, LANES, own_blocks), F32),
            pltpu.VMEM((3, own_blocks, 3, LANES), F32),
            pltpu.VMEM((WIDTH, LANES), jnp.int32),
            pltpu.VMEM((groups, WIDTH, LANES), jnp.int32),
            pltpu.VMEM((groups, WIDTH, LANES), jnp.int32),
            pltpu.VMEM((groups, WIDTH, LANES), jnp.int32),
            pltpu.VMEM((groups, WIDTH, WIDTH, LANES), F32),
            pltpu.VMEM((wide, groups * LANES), BF16),
            pltpu.VMEM((groups * LANES, wide), BF16),
            pltpu.VMEM((groups, 3 * LANES, LANES), F32),
            pltpu.VMEM((3, WIDTH, LANES), F32),
            pltpu.VMEM((2, 3 * LANES, groups * LANES), BF16),
            pltpu.VMEM((2, 3 * LANES, wide), BF16),
            pltpu.VMEM((3 * LANES, own_blocks), F32),
            pltpu.VMEM((LANES, own_blocks), F32),
            pltpu.VMEM((steps, 2 * LANES, LANES), BF16),
            pltpu.VMEM((steps, LANES, 2 * LANES), BF16),
            pltpu.VMEM((steps, 2 * LANES, LANES), BF16),
            pltpu.VMEM((steps, LANES, 2 * LANES), BF16),
            pltpu.VMEM((devices * 8, LANES), F32),
            pltpu.VMEM((devices * 8, LANES), F32),
            pltpu.VMEM((devices * ROWS, LANES), F32),
            pltpu.VMEM((steps, devices * ROWS, LANES), F32),
            pltpu.VMEM((48, LANES), F32),
            pltpu.VMEM((steps, 48, LANES), F32),
            pltpu.VMEM((48, LANES), F32),
            pltpu.VMEM((steps, 48, LANES), F32),
            dma((3,)),
            dma((groups,)),
            dma,
            dma,
            dma((steps,)),
            dma((steps,)),
            dma((steps,)),
            dma((steps,)),
            dma((steps,)),
            dma((steps,)),
        ],
        compiler_params=pltpu.CompilerParams(
            collective_id=0, has_side_effects=True, vmem_limit_bytes=62 * 2**20
        ),
    )(
        turned(displacement),
        turned(velocity),
        turned(load),
        mass.reshape(own_blocks, LANES),
        stiffness,
        connectivity,
        clearance,
        match_device.transpose(0, 2, 1),
        match_slot,
    )

    def restored(array):
        return array.transpose(1, 0, 2).reshape(3, own_blocks * LANES)

    return restored(deform), restored(motion)


def solution(mesh):
    return jax.shard_map(
        body,
        mesh=mesh,
        in_specs=(
            P(None, ("circ", "xsec")),
            P(None, ("circ", "xsec")),
            P(None, ("circ", "xsec")),
            P(("circ", "xsec")),
            P(None, None, ("circ", "xsec")),
            P(None, ("circ", "xsec")),
            P(("circ", "xsec"), None),
            P(None, ("circ", "xsec"), None),
            P(None, ("circ", "xsec")),
        ),
        out_specs=(P(None, ("circ", "xsec")), P(None, ("circ", "xsec"))),
        check_vma=False,
    )
```

```python
import functools

import jax
import jax.numpy as jnp
from jax import lax
from jax.experimental import pallas as pl
from jax.experimental.pallas import tpu as pltpu
from jax.sharding import PartitionSpec as P

FACE = 1024
WIDTH = 64
LANES = 128
ROWS = 16
PENALTY = 4.0
DASHPOT = 1.0
FRICTION = 2.0
TIMESTEP = 0.25
BF16 = jnp.bfloat16
F32 = jnp.float32
MESH = pl.DeviceIdType.MESH


def halves(x):
    first = x.astype(BF16)
    return first, (x - first.astype(F32)).astype(BF16)


def one_hot(mask):
    return jnp.where(mask, 1.0, 0.0).astype(BF16)


def dot(a, b):
    return jnp.dot(a, b, preferred_element_type=F32)


def iota(shape, dim):
    return lax.broadcasted_iota(jnp.int32, shape, dim)


def padded_transpose(block):
    rows = block.shape[0]
    return jnp.concatenate([block, jnp.zeros((LANES - rows, LANES), F32)], axis=0).T


def contact_terms(cycle, groove):
    relative = [cycle[k] - groove[k] for k in range(3)]
    intersection = jnp.maximum(relative[0], 0.0)
    closing = cycle[3] - groove[3]
    return [
        intersection * (PENALTY + DASHPOT * closing),
        FRICTION * intersection * relative[1],
        FRICTION * intersection * relative[2],
    ]


def column_of(block, own_blocks, face_blocks):
    upper = own_blocks + face_blocks
    return jnp.where(
        block < face_blocks,
        block + own_blocks,
        jnp.where(block >= upper, block + 2 * face_blocks, block - face_blocks),
    )


def fill_tables(conn_ref, pick_ref, back_ref, own_blocks, face_blocks):
    groups = conn_ref.shape[1] // LANES
    columns = pick_ref.shape[0]
    for group in range(groups):
        row = column_of(conn_ref[0:1, group * LANES : (group + 1) * LANES] >> 7, own_blocks, face_blocks)
        pick_ref[:, group * LANES : (group + 1) * LANES] = one_hot(iota((columns, LANES), 0) == row)
        col = jnp.broadcast_to(row, (LANES, LANES)).astype(F32).T[:, :1].astype(jnp.int32)
        back_ref[group * LANES : (group + 1) * LANES, :] = one_hot(iota((LANES, columns), 1) == col)


def gather_tiles(state_ref, pick_ref, tile_ref):
    groups = tile_ref.shape[0]
    for pair in range(groups // 2):
        pick = pick_ref[:, pair * 256 : (pair + 1) * 256]
        found = dot(state_ref[0], pick) + dot(state_ref[1], pick)
        tile_ref[2 * pair] = found[:, :LANES]
        tile_ref[2 * pair + 1] = found[:, LANES:]


def pick_rows(table, index):
    out = []
    for j in range(0, WIDTH, 8):
        low = index[j : j + 8] & 7
        high = index[j : j + 8] >> 3
        value = jnp.take_along_axis(table[0:8], low, axis=0, mode="promise_in_bounds")
        for m in range(1, WIDTH // 8):
            other = jnp.take_along_axis(
                table[m * 8 : m * 8 + 8], low, axis=0, mode="promise_in_bounds"
            )
            value = jnp.where(high == m, other, value)
        out.append(value)
    return jnp.concatenate(out, axis=0)


def running_sums(rows):
    at = iota((8, LANES), 0)
    base = jnp.zeros((1, LANES), F32)
    out = []
    for j in range(0, WIDTH, 8):
        piece = rows[j : j + 8]
        for by in (1, 2, 4):
            piece = piece + jnp.where(at >= by, pltpu.roll(piece, by, 0), 0.0)
        piece = piece + base
        base = piece[7:8]
        out.append(piece)
    return jnp.concatenate(out, axis=0)


def sort_links(group, link_ref, key_ref, order_ref, end_ref):
    at = iota((WIDTH, LANES), 0)
    local = link_ref[group] & 63
    keys = local * WIDTH + at
    key_ref[...] = keys

    def count(i, carry):
        place, end = carry
        key = key_ref[pl.ds(i, 1), :]
        place = place + jnp.where(key < keys, 1, 0)
        end = end + jnp.where(key < (at + 1) * WIDTH, 1, 0)
        return place, end

    zero = jnp.zeros((WIDTH, LANES), jnp.int32)
    place, end = lax.fori_loop(0, WIDTH, count, (zero, zero), unroll=4)
    end_ref[group] = end
    key_ref[...] = place

    def invert(i, order):
        return jnp.where(key_ref[pl.ds(i, 1), :] == at, i, order)

    order_ref[group] = lax.fori_loop(0, WIDTH, invert, zero, unroll=4)


def element_group(group, stiff_ref, link_ref, order_ref, end_ref, tile_ref, row_ref, spread_ref):
    links = link_ref[group]
    odd = ((links[0:1, :] >> 6) & 1) == 1
    local = links & 63
    near = []
    for c in range(3):
        tile = jnp.where(
            odd,
            tile_ref[group, c * 128 + 64 : c * 128 + 128, :],
            tile_ref[group, c * 128 : c * 128 + 64, :],
        )
        near.append(pick_rows(tile, local))

    def row(i, carry):
        stiff = stiff_ref[group, i]
        for c in range(3):
            row_ref[c, pl.ds(i, 1), :] = jnp.sum(stiff * near[c], axis=0, keepdims=True)
        return carry

    lax.fori_loop(0, WIDTH, row, 0, unroll=8)
    order = order_ref[group]
    end = end_ref[group]
    last = jnp.maximum(end - 1, 0)
    at = pl.ds(pl.multiple_of(group * LANES, LANES), LANES)
    for c in range(3):
        totals = pick_rows(running_sums(pick_rows(row_ref[c], order)), last)
        totals = jnp.where(end > 0, totals, 0.0)
        before = jnp.where(iota((WIDTH, LANES), 0) > 0, pltpu.roll(totals, 1, 0), 0.0)
        sums = totals - before
        for half in range(2):
            kept = jnp.where(odd if half else jnp.logical_not(odd), sums, 0.0)
            for p, part in enumerate(halves(kept)):
                spread_ref[p, c * 128 + half * 64 : c * 128 + half * 64 + 64, at] = part


def kernel(
    counts, disp_in, vel_in, load_in, mass_ref, stiff_hbm, conn_ref, clear_ref,
    target_ref, slot_ref, disp_out, vel_out,
    disp_ref, vel_ref, load_ref, given_ref, key_ref, order_ref, end_ref, link_ref, stiff_ref, pick_ref, back_ref, tile_ref, near_ref, spread_ref, state_ref, force_ref, scale_ref,
    pickers, pickers_t, seers, seers_t, note_out, note_in, send_ref, recv_ref,
    face_out, face_in, edge_out, edge_in,
    given_sem, stiff_sem, note_send, note_recv, block_send, block_recv, face_send, face_recv, edge_send,
    edge_recv,
):
    circ_count, xsec_count, steps, own_blocks, face_blocks = counts
    devices = circ_count * xsec_count
    groups = stiff_ref.shape[0]
    circ, xsec = lax.axis_index("circ"), lax.axis_index("xsec")
    me = circ * xsec_count + xsec
    lower = (lax.rem(circ + circ_count - 1, circ_count), xsec)
    upper = (lax.rem(circ + 1, circ_count), xsec)

    def peer(r):
        other = lax.rem(me + r, devices)
        return other, (other // xsec_count, lax.rem(other, xsec_count))

    given = [
        pltpu.make_async_copy(source, given_ref.at[i], given_sem.at[i])
        for i, source in enumerate((disp_in, vel_in, load_in))
    ]
    for copy in given:
        copy.start()
    copies = [
        pltpu.make_async_copy(
            stiff_hbm.at[:, :, pl.ds(g * LANES, LANES)], stiff_ref.at[g], stiff_sem.at[g]
        )
        for g in range(groups)
    ]
    for copy in copies:
        copy.start()

    barrier = pltpu.get_barrier_semaphore()

    def greet(r, carry):
        pl.semaphore_signal(barrier, inc=1, device_id=peer(r)[1], device_id_type=MESH)
        return carry

    lax.fori_loop(1, devices, greet, 0)

    square = (LANES, LANES)
    note = jnp.zeros(square, F32)
    for s in range(steps):
        dev_row = target_ref[s]
        dev_square = jnp.broadcast_to(dev_row, square)
        dev_col = dev_square.astype(F32).T.astype(jnp.int32)
        earlier = (dev_col == dev_square) & (iota(square, 0) < iota(square, 1))
        rank_row = jnp.sum(jnp.where(earlier, 1.0, 0.0), axis=0, keepdims=True).astype(jnp.int32)
        code_row = jnp.broadcast_to(dev_row + rank_row * devices, square)
        code_col = code_row.astype(F32).T.astype(jnp.int32)
        for r in range(2):
            mine = code_row == iota(square, 0) + r * devices
            pickers[s, r * LANES : (r + 1) * LANES, :] = one_hot(mine)
            pickers_t[s, :, r * LANES : (r + 1) * LANES] = one_hot(
                code_col == iota(square, 1) + r * devices
            )
            named = jnp.where(mine, (slot_ref[s : s + 1, :] + 1).astype(F32), 0.0)
            named = jnp.sum(named, axis=1, keepdims=True)
            note = note + jnp.where(iota(square, 1) == 2 * s + r, named, 0.0)
    note_out[...] = jnp.zeros(note_out.shape, F32)
    note_out[pl.ds(0, LANES, stride=8), :] = note

    for i, ref in enumerate((disp_ref, vel_ref, load_ref)):
        given[i].wait()
        for c in range(3):
            ref[c] = given_ref[i, :, c, :].T
    scale_ref[...] = TIMESTEP / mass_ref[...].T

    pl.semaphore_wait(barrier, devices - 1)

    def tell(r, carry):
        other, where = peer(r)
        pltpu.make_async_remote_copy(
            src_ref=note_out.at[pl.ds(pl.multiple_of(other * 8, 8), 8)],
            dst_ref=note_in.at[pl.ds(pl.multiple_of(me * 8, 8), 8)],
            send_sem=note_send,
            recv_sem=note_recv,
            device_id=where,
            device_id_type=MESH,
        ).start()
        return carry

    lax.fori_loop(1, devices, tell, 0)
    home = pl.ds(pl.multiple_of(me * 8, 8), 8)
    note_in[home, :] = note_out[home, :]

    for group in range(groups):
        link_ref[group] = conn_ref[:, group * LANES : (group + 1) * LANES]
    fill_tables(conn_ref, pick_ref, back_ref, own_blocks, face_blocks)

    def sort_step(group, carry):
        sort_links(group, link_ref, key_ref, order_ref, end_ref)
        return carry

    lax.fori_loop(0, groups, sort_step, 0)

    told = note_in.at[pl.ds(0, (devices - 1) * 8)]
    pltpu.make_async_copy(told, told, note_recv).wait()
    pltpu.make_async_copy(told, told, note_send).wait()
    heard = note_in[pl.ds(0, LANES, stride=8), :]
    heard_t = heard.T
    for s in range(steps):
        for r in range(2):
            q = 2 * s + r
            seers[s, r * LANES : (r + 1) * LANES, :] = one_hot(
                heard[:, q : q + 1] == (iota(square, 1) + 1).astype(F32)
            )
            seers_t[s, :, r * LANES : (r + 1) * LANES] = one_hot(
                heard_t[q : q + 1, :] == (iota(square, 0) + 1).astype(F32)
            )
    for copy in copies:
        copy.wait()

    surface = LANES
    groove = own_blocks - surface
    lane = iota(square, 1)

    def step(s, carry):
        cycle = [disp_ref[c][:, :surface].T for c in range(3)] + [vel_ref[0][:, :surface].T]
        mate = [disp_ref[c][:, groove:].T for c in range(3)] + [vel_ref[0][:, groove:].T]
        for c in range(3):
            face_out[c * 8 : c * 8 + 8, :] = cycle[c][:8]
            face_out[24 + c * 8 : 24 + c * 8 + 8, :] = mate[c][LANES - 8 :]
        faces = []
        for side, where in ((0, lower), (1, upper)):
            faces.append(
                pltpu.make_async_remote_copy(
                    src_ref=face_out.at[pl.ds(side * 24, 24)],
                    dst_ref=face_in.at[s, pl.ds((1 - side) * 24, 24)],
                    send_sem=face_send.at[s],
                    recv_sem=face_recv.at[s],
                    device_id=where,
                    device_id_type=MESH,
                )
            )
        for copy in faces:
            copy.start()
        mate[0] = mate[0] + clear_ref[...]

        for base, table, data in ((0, pickers, cycle), (8, seers, mate)):
            pieces = halves(jnp.concatenate(data, axis=1))
            packed = sum(dot(table[s], piece) for piece in pieces)
            for r in range(2):
                for k in range(4):
                    send_ref[pl.ds(base + r * 4 + k, LANES, stride=ROWS), :] = packed[
                        r * LANES : (r + 1) * LANES, k * LANES : (k + 1) * LANES
                    ]

        def ship(r, inner):
            other, where = peer(r)
            pltpu.make_async_remote_copy(
                src_ref=send_ref.at[pl.ds(pl.multiple_of(other * ROWS, ROWS), ROWS)],
                dst_ref=recv_ref.at[s, pl.ds(pl.multiple_of(me * ROWS, ROWS), ROWS)],
                send_sem=block_send.at[s],
                recv_sem=block_recv.at[s],
                device_id=where,
                device_id_type=MESH,
            ).start()
            return inner

        lax.fori_loop(1, devices, ship, 0)
        own_rows = pl.ds(pl.multiple_of(me * ROWS, ROWS), ROWS)
        recv_ref[s, own_rows, :] = send_ref[own_rows, :]

        for c in range(3):
            for p, piece in enumerate(halves(disp_ref[c])):
                state_ref[p, c * LANES : (c + 1) * LANES, :own_blocks] = piece
        both = face_in.at[s]
        pltpu.make_async_copy(both, both, face_recv.at[s]).wait()
        halo = padded_transpose(face_in[s])
        for c in range(3):
            turned = pltpu.roll(halo, LANES - 8 * c, 1) if c else halo
            for p, piece in enumerate(halves(turned)):
                state_ref[p, c * LANES : (c + 1) * LANES, own_blocks:] = piece

        gather_tiles(state_ref, pick_ref, tile_ref)

        def group_step(group, inner):
            element_group(
                group, stiff_ref, link_ref, order_ref, end_ref, tile_ref, near_ref, spread_ref
            )
            return inner

        lax.fori_loop(0, groups, group_step, 0)
        tails = dot(spread_ref[0], back_ref[:, own_blocks:]) + dot(
            spread_ref[1], back_ref[:, own_blocks:]
        )

        edge = jnp.zeros(square, F32)
        for c in range(3):
            tail = tails[c * LANES : (c + 1) * LANES]
            turned = pltpu.roll(tail, 8 * c, 1) if c else tail
            here = ((lane >= 8 * c) & (lane < 8 * c + 8)) | (
                (lane >= 24 + 8 * c) & (lane < 32 + 8 * c)
            )
            edge = jnp.where(here, turned, edge)
        edge_out[...] = edge.T[:48]
        for side, where in ((0, lower), (1, upper)):
            pltpu.make_async_remote_copy(
                src_ref=edge_out.at[pl.ds(side * 24, 24)],
                dst_ref=edge_in.at[s, pl.ds((1 - side) * 24, 24)],
                send_sem=edge_send.at[s],
                recv_sem=edge_recv.at[s],
                device_id=where,
                device_id_type=MESH,
            ).start()

        force_ref[...] = dot(spread_ref[0], back_ref[:, :own_blocks]) + dot(
            spread_ref[1], back_ref[:, :own_blocks]
        )
        arrived = recv_ref.at[s, pl.ds(0, (devices - 1) * ROWS)]
        pltpu.make_async_copy(arrived, arrived, block_recv.at[s]).wait()

        def rows_of(ref, base, r):
            return [ref[pl.ds(base + r * 4 + k, LANES, stride=ROWS), :] for k in range(4)]

        incoming = recv_ref.at[s]
        on_groove, on_cycle = [], []
        for r in range(2):
            on_groove.append(
                jnp.concatenate(
                    contact_terms(rows_of(incoming, 0, r), rows_of(send_ref, 8, r)), axis=1
                )
            )
            on_cycle.append(
                jnp.concatenate(
                    contact_terms(rows_of(send_ref, 0, r), rows_of(incoming, 8, r)), axis=1
                )
            )
        groove_force = sum(
            dot(seers_t[s], piece) for piece in halves(jnp.concatenate(on_groove, axis=0))
        )
        cycle_force = sum(
            dot(pickers_t[s], piece) for piece in halves(jnp.concatenate(on_cycle, axis=0))
        )

        both = edge_in.at[s]
        pltpu.make_async_copy(both, both, edge_recv.at[s]).wait()
        edge = padded_transpose(edge_in[s])
        for c in range(3):
            span = slice(c * LANES, (c + 1) * LANES)
            first = pltpu.roll(edge, LANES - 8 * c, 1) if c else edge
            last = pltpu.roll(edge, 96 - 8 * c, 1)
            extra = (
                -cycle_force[:, span].T - jnp.where(lane < 8, first, 0.0),
                None,
                groove_force[:, span].T - jnp.where(lane >= LANES - 8, last, 0.0),
            )
            for low, high, add in (
                (0, surface, extra[0]),
                (surface, groove, None),
                (groove, own_blocks, extra[2]),
            ):
                at = slice(low, high)
                pull = load_ref[c][:, at] - force_ref[span, at]
                if add is not None:
                    pull = pull + add
                speed = vel_ref[c, :, at] + pull * scale_ref[:, at]
                vel_ref[c, :, at] = speed
                disp_ref[c, :, at] = disp_ref[c, :, at] + TIMESTEP * speed

        sent = send_ref.at[pl.ds(0, (devices - 1) * ROWS)]
        pltpu.make_async_copy(sent, sent, block_send.at[s]).wait()
        pltpu.make_async_copy(face_out, face_out, face_send.at[s]).wait()
        pltpu.make_async_copy(edge_out, edge_out, edge_send.at[s]).wait()
        return carry

    lax.fori_loop(0, steps, step, 0)
    for c in range(3):
        given_ref[0, :, c, :] = disp_ref[c].T
        given_ref[1, :, c, :] = vel_ref[c].T
    back = [
        pltpu.make_async_copy(given_ref.at[i], out, given_sem.at[i])
        for i, out in enumerate((disp_out, vel_out))
    ]
    for copy in back:
        copy.start()
    for copy in back:
        copy.wait()


def body(
    displacement, velocity, load, mass, stiffness, connectivity, clearance, match_device, match_slot
):
    steps = match_slot.shape[0]
    circ_count, xsec_count = lax.axis_size("circ"), lax.axis_size("xsec")
    devices = circ_count * xsec_count
    own_blocks = displacement.shape[1] // LANES
    face_blocks = FACE // LANES
    groups = stiffness.shape[2] // LANES
    wide = own_blocks + LANES

    def turned(array):
        return array.reshape(3, own_blocks, LANES).transpose(1, 0, 2)

    vm = pl.BlockSpec(memory_space=pltpu.VMEM)
    far = pl.BlockSpec(memory_space=pl.ANY)
    shape = jax.ShapeDtypeStruct((own_blocks, 3, LANES), F32)
    dma = pltpu.SemaphoreType.DMA
    deform, motion = pl.pallas_call(
        functools.partial(kernel, (circ_count, xsec_count, steps, own_blocks, face_blocks)),
        out_shape=(shape, shape),
        in_specs=[far, far, far, vm, far, vm, vm, vm, vm],
        out_specs=(far, far),
        scratch_shapes=[
            pltpu.VMEM((3, LANES, own_blocks), F32),
            pltpu.VMEM((3, LANES, own_blocks), F32),
            pltpu.VMEM((3, LANES, own_blocks), F32),
            pltpu.VMEM((3, own_blocks, 3, LANES), F32),
            pltpu.VMEM((WIDTH, LANES), jnp.int32),
            pltpu.VMEM((groups, WIDTH, LANES), jnp.int32),
            pltpu.VMEM((groups, WIDTH, LANES), jnp.int32),
            pltpu.VMEM((groups, WIDTH, LANES), jnp.int32),
            pltpu.VMEM((groups, WIDTH, WIDTH, LANES), F32),
            pltpu.VMEM((wide, groups * LANES), BF16),
            pltpu.VMEM((groups * LANES, wide), BF16),
            pltpu.VMEM((groups, 3 * LANES, LANES), F32),
            pltpu.VMEM((3, WIDTH, LANES), F32),
            pltpu.VMEM((2, 3 * LANES, groups * LANES), BF16),
            pltpu.VMEM((2, 3 * LANES, wide), BF16),
            pltpu.VMEM((3 * LANES, own_blocks), F32),
            pltpu.VMEM((LANES, own_blocks), F32),
            pltpu.VMEM((steps, 2 * LANES, LANES), BF16),
            pltpu.VMEM((steps, LANES, 2 * LANES), BF16),
            pltpu.VMEM((steps, 2 * LANES, LANES), BF16),
            pltpu.VMEM((steps, LANES, 2 * LANES), BF16),
            pltpu.VMEM((devices * 8, LANES), F32),
            pltpu.VMEM((devices * 8, LANES), F32),
            pltpu.VMEM((devices * ROWS, LANES), F32),
            pltpu.VMEM((steps, devices * ROWS, LANES), F32),
            pltpu.VMEM((48, LANES), F32),
            pltpu.VMEM((steps, 48, LANES), F32),
            pltpu.VMEM((48, LANES), F32),
            pltpu.VMEM((steps, 48, LANES), F32),
            dma((3,)),
            dma((groups,)),
            dma,
            dma,
            dma((steps,)),
            dma((steps,)),
            dma((steps,)),
            dma((steps,)),
            dma((steps,)),
            dma((steps,)),
        ],
        compiler_params=pltpu.CompilerParams(
            collective_id=0, has_side_effects=True, vmem_limit_bytes=62 * 2**20
        ),
    )(
        turned(displacement),
        turned(velocity),
        turned(load),
        mass.reshape(own_blocks, LANES),
        stiffness,
        connectivity,
        clearance,
        match_device.transpose(0, 2, 1),
        match_slot,
    )

    def restored(array):
        return array.transpose(1, 0, 2).reshape(3, own_blocks * LANES)

    return restored(deform), restored(motion)


def solution(mesh):
    return jax.shard_map(
        body,
        mesh=mesh,
        in_specs=(
            P(None, ("circ", "xsec")),
            P(None, ("circ", "xsec")),
            P(None, ("circ", "xsec")),
            P(("circ", "xsec")),
            P(None, None, ("circ", "xsec")),
            P(None, ("circ", "xsec")),
            P(("circ", "xsec"), None),
            P(None, ("circ", "xsec"), None),
            P(None, ("circ", "xsec")),
        ),
        out_specs=(P(None, ("circ", "xsec")), P(None, ("circ", "xsec"))),
        check_vma=False,
    )
```
